32 devices in a mesh: groups: 2 (over y), seq: 4 (over z), head: 4 (over x, core).
Axes of the slice: x: 2, y: 2, z: 4, core: 2. Of those that a mesh axis runs over, the one named last changes fastest.
Arguments:
- hidden: bfloat16 [2048, 2560], P(('groups', 'seq'), 'head'), parts along dimension 0, may hold values from -6 to 6
- w_zx: bfloat16 [2560, 2, 3072], P('seq', None, 'head'), may hold values from -0.125 to 0.125
- w_dt: bfloat16 [2560, 48], P('seq', 'head'), may hold values from -0.125 to 0.125
- w_bc: bfloat16 [2560, 2, 128], P('seq'), may hold values from -0.125 to 0.125
- dt_bias: float32 [48], P('head'), may hold values from -1 to 0
- a_log: float32 [48], P('head'), may hold values from -12 to -2, as said below
- d_skip: float32 [48], P('head'), may hold values from 0.5 to 1.5
- norm_gain: float32 [3072], P('head'), may hold values from 0.5 to 1.5
- w_out: bfloat16 [3072, 2560], P('head', 'seq'), may hold values from -0.109375 to 0.109375
- grad_out: bfloat16 [2048, 2560], P(('groups', 'seq'), 'head'), parts along dimension 0, may hold values from -6 to 6
Outputs:
- layer_out: bfloat16 [2048, 2560], P(('groups', 'seq'), 'head'), parts along dimension 0
- grad_hidden: bfloat16 [2048, 2560], P(('groups', 'seq'), 'head'), parts along dimension 0
- grad_wzx: float32 [5120, 2, 3072], P(('groups', 'seq'), None, 'head'), parts along dimension 0
- grad_wdt: float32 [5120, 48], P(('groups', 'seq'), 'head'), parts along dimension 0
- grad_wbc: float32 [5120, 2, 128], P(('groups', 'seq')), parts along dimension 0
- grad_dtbias: float32 [96], P(('groups', 'head')), parts along dimension 0
- grad_alog: float32 [96], P(('groups', 'head')), parts along dimension 0
- grad_dskip: float32 [96], P(('groups', 'head')), parts along dimension 0
- grad_gain: float32 [6144], P(('groups', 'head')), parts along dimension 0
- grad_wout: float32 [6144, 2560], P(('groups', 'head'), 'seq'), parts along dimension 0
The draws below stay inside these ranges and needn't reach their ends.
There are 2 independent parts, one for each index of `groups`. The reference program is written for one: setup_inputs(seed, part) draws one part's arguments, and reference() takes and returns one part's arrays. A program takes and returns all parts, laid end to end along the dimension named above; an argument that names none is the same for every part. Nothing has to cross between parts.
Inputs may be any that keep to these rules, and one draw needn't show every extreme that they name: `a_log`: log of each head's decay rate.
All inputs are finite; a program needn't handle non-finite values.
Results may differ from the reference program's by a relative error of at most 0.029.
Values may be sent and summed in bfloat16 or wider, within the bound.
A program may use at most 128 MiB of HBM per device.

```python
import jax
import jax.numpy as jnp
from jax import lax

D = 2560
HEADS = 48
HDIM = 64
STATE = 128
BLOCK = 128
L_DEV = 256
SEQLEN = 1024
DI = 3072
N_SEQ = 4
N_HEAD = 4


def draw_a_log(key, part):
    pick_key, slow_key, fast_key = jax.random.split(jax.random.fold_in(key, 17), 3)
    share = 0.5
    slow_mask = jax.random.uniform(pick_key, (HEADS,)) < share
    slow_rate = jnp.exp(jax.random.uniform(slow_key, (HEADS,), minval=jnp.log(0.8 / SEQLEN), maxval=jnp.log(2.0 / SEQLEN)))
    fast_rate = jnp.exp(jax.random.uniform(fast_key, (HEADS,), minval=jnp.log(1.0 / 50.0), maxval=jnp.log(1.0 / 30.0)))
    return jnp.log(jnp.where(slow_mask, slow_rate, fast_rate) / 0.6).astype(jnp.float32)


def steps_of(stream_key, dims, cuts, low, top_value):
    level = 1.0
    for axis_at, blocks in cuts:
        steps = jax.random.uniform(jax.random.fold_in(jax.random.fold_in(stream_key, 6), axis_at), (blocks,), jnp.float32, low / len(cuts), top_value / len(cuts))
        level = level * jnp.repeat(jnp.exp(steps), dims[axis_at] // blocks).reshape((-1,) + (1,) * (len(dims) - 1 - axis_at))
    return level


def bell_draw(key, extent, deviation, most, pieces=(), kind=jnp.bfloat16):
    array = jax.random.normal(key, extent, jnp.float32) * deviation
    if len(pieces) > 0:
        array = steps_of(key, extent, pieces, -0.22, 0.18) * array
    return jnp.clip(array, min=-most, max=most).astype(kind)


def setup_inputs(seed: int = 0, part: int = 0) -> dict:
    keys = jax.random.split(jax.random.key(seed), 11)
    part_keys = jax.random.split(jax.random.fold_in(keys[10], part), 11)
    hidden = bell_draw(part_keys[0], (SEQLEN, D), 1.0, 6.0, ((0, 4), (1, 4)))
    w_zx = bell_draw(keys[1], (D, 2, DI), D ** -0.5, 0.125, ((0, 4), (2, 4)))
    w_dt = bell_draw(keys[2], (D, HEADS), D ** -0.5, 0.125, ((0, 4), (1, 4)))
    w_bc = bell_draw(keys[3], (D, 2, STATE), D ** -0.5, 0.125, ((0, 4),))
    dt_bias = jnp.clip(-1.0 + 1.0 * jax.random.uniform(keys[4], (HEADS,), jnp.float32) ** steps_of(keys[4], (HEADS,), ((0, 4),), -0.2, 0.2), -1.0, 0.0)
    a_log = draw_a_log(jax.random.fold_in(keys[10], 71), part)
    d_skip = jnp.clip(0.5 + 1.0 * jax.random.uniform(keys[6], (HEADS,), jnp.float32) ** steps_of(keys[6], (HEADS,), ((0, 4),), -0.2, 0.2), 0.5, 1.5)
    norm_gain = jnp.clip(1.0 + 0.1 * jax.random.normal(keys[7], (DI,), jnp.float32), 0.5, 1.5)
    w_out = bell_draw(keys[8], (DI, D), DI ** -0.5, 0.109375, ((0, 4), (1, 4)))
    grad_out = bell_draw(part_keys[9], (SEQLEN, D), 1.0, 6.0, ((0, 4), (1, 4)))
    return dict(hidden=hidden, w_zx=w_zx, w_dt=w_dt, w_bc=w_bc, dt_bias=dt_bias, a_log=a_log, d_skip=d_skip, norm_gain=norm_gain, w_out=w_out, grad_out=grad_out)


EPS_NORM = 1e-05
HIGH = lax.Precision.HIGHEST

def split_inputs(zx_f, dtr_f, bc_f, dt_bias, a_log):
    rows = dtr_f.shape[0]
    nheads = dtr_f.shape[1]
    width = zx_f.shape[2] // nheads
    z_gate = zx_f[:, 0]
    x_in = jax.nn.silu(zx_f[:, 1]).reshape(rows, nheads, width)
    dt_val = jax.nn.softplus(dtr_f + dt_bias[None])
    log_decay = -dt_val * jnp.exp(a_log)[None]
    return (z_gate, x_in, dt_val, log_decay, bc_f[:, 0], bc_f[:, 1])

def ssd_pass(x_in, dt_val, log_decay, b_in, c_in, d_skip, s_init, with_out):
    rows, nheads, width = x_in.shape
    blocks = rows // BLOCK
    lower = jnp.arange(BLOCK)[:, None] >= jnp.arange(BLOCK)[None, :]
    parts = (x_in.reshape(blocks, BLOCK, nheads, width), dt_val.reshape(blocks, BLOCK, nheads), log_decay.reshape(blocks, BLOCK, nheads), b_in.reshape(blocks, BLOCK, -1), c_in.reshape(blocks, BLOCK, -1))

    def advance(state, block):
        x_blk, dt_blk, ld_blk, b_blk, c_blk = block
        cumul = jnp.cumsum(ld_blk, axis=0)
        tail = cumul[-1]
        inflow = jnp.exp(tail[None] - cumul) * dt_blk
        fresh = state * jnp.exp(tail)[:, None, None] + jnp.einsum('sh,shp,sn->hpn', inflow, x_blk, b_blk, precision=HIGH)
        if not with_out:
            return (fresh, None)
        scores = jnp.dot(c_blk, b_blk.T, precision=HIGH)
        gaps = cumul.T[:, :, None] - cumul.T[:, None, :]
        weights = jnp.exp(jnp.where(lower[None], gaps, -1e+30)) * scores[None] * dt_blk.T[:, None, :]
        y_blk = jnp.einsum('hts,shp->thp', weights, x_blk, precision=HIGH)
        y_blk = y_blk + jnp.einsum('tn,hpn->thp', c_blk, state, precision=HIGH) * jnp.exp(cumul)[:, :, None]
        y_blk = y_blk + d_skip[None, :, None] * x_blk
        return (fresh, y_blk)
    final, outs = lax.scan(advance, s_init, parts)
    return (outs, final)

def mixer(zx_f, dtr_f, bc_f, dt_bias, a_log, d_skip, s_init):
    z_gate, x_in, dt_val, log_decay, b_in, c_in = split_inputs(zx_f, dtr_f, bc_f, dt_bias, a_log)
    outs, final = ssd_pass(x_in, dt_val, log_decay, b_in, c_in, d_skip, s_init, True)
    return outs.reshape(z_gate.shape[0], -1) * jax.nn.silu(z_gate)

def core(zx_f, dtr_f, bc_f, dt_bias, a_log, d_skip, norm_gain):
    start_state = jnp.zeros((dt_bias.shape[0], HDIM, STATE), zx_f.dtype)
    mixed = mixer(zx_f, dtr_f, bc_f, dt_bias, a_log, d_skip, start_state)
    rinv = lax.rsqrt(lax.optimization_barrier(jnp.mean(mixed * mixed, axis=1)) + EPS_NORM)
    return (mixed * rinv[:, None] * norm_gain[None]).astype(jnp.bfloat16)

def rounded(value):
    return lax.optimization_barrier(value.astype(jnp.bfloat16)).astype(jnp.float32)

def split_pair(value):
    upper = value.astype(jnp.bfloat16)
    lower_part = (value - upper.astype(value.dtype)).astype(jnp.bfloat16)
    return (upper, lower_part)

def reference(hidden, w_zx, w_dt, w_bc, dt_bias, a_log, d_skip, norm_gain, w_out, grad_out):
    total = hidden.shape[0]
    wide = HEADS * HDIM
    zx_b = jnp.dot(hidden, w_zx.reshape(D, 2 * wide), preferred_element_type=jnp.float32).astype(jnp.bfloat16)
    dtr_b = jnp.dot(hidden, w_dt, preferred_element_type=jnp.float32).astype(jnp.bfloat16)
    bc_b = jnp.dot(hidden, w_bc.reshape(D, 2 * STATE), preferred_element_type=jnp.float32).astype(jnp.bfloat16)
    zx_b, dtr_b, bc_b = lax.optimization_barrier((zx_b, dtr_b, bc_b))
    zx_f = zx_b.astype(jnp.float32).reshape(total, 2, wide)
    dtr_f = dtr_b.astype(jnp.float32)
    bc_f = bc_b.astype(jnp.float32).reshape(total, 2, STATE)
    gated, pull = jax.vjp(core, zx_f, dtr_f, bc_f, dt_bias, a_log, d_skip, norm_gain)
    group = wide // N_HEAD
    layer_sum = jnp.zeros((total, D), jnp.float32)
    for index in range(N_HEAD):
        part = jnp.dot(gated[:, index * group:(index + 1) * group], w_out[index * group:(index + 1) * group], preferred_element_type=jnp.float32)
        layer_sum = layer_sum + rounded(part)
    layer_out = layer_sum.astype(jnp.bfloat16)
    grad_gated = jnp.dot(grad_out, w_out.T, preferred_element_type=jnp.float32).astype(jnp.bfloat16)
    d_zx, d_dtr, d_bc, grad_dtbias, grad_alog, grad_dskip, grad_gain = pull(grad_gated)
    d_zx = d_zx.reshape(total, 2 * wide).astype(jnp.bfloat16)
    d_dtr = d_dtr.astype(jnp.bfloat16)
    d_bc = d_bc.reshape(total, 2 * STATE)
    bc_upper, bc_lower = split_pair(d_bc)
    flat_bc = w_bc.reshape(D, 2 * STATE)
    grad_hidden = (jnp.dot(d_zx, w_zx.reshape(D, 2 * wide).T, preferred_element_type=jnp.float32) + jnp.dot(d_dtr, w_dt.T, preferred_element_type=jnp.float32) + jnp.dot(bc_upper, flat_bc.T, preferred_element_type=jnp.float32) + jnp.dot(bc_lower, flat_bc.T, preferred_element_type=jnp.float32)).astype(jnp.bfloat16)

    def accumulate(index, sums):
        begin = index * L_DEV
        h_s = lax.dynamic_slice_in_dim(hidden, begin, L_DEV, 0)
        zx_s = lax.dynamic_slice_in_dim(d_zx, begin, L_DEV, 0)
        dt_s = lax.dynamic_slice_in_dim(d_dtr, begin, L_DEV, 0)
        hi_s = lax.dynamic_slice_in_dim(bc_upper, begin, L_DEV, 0)
        lo_s = lax.dynamic_slice_in_dim(bc_lower, begin, L_DEV, 0)
        g_s = lax.dynamic_slice_in_dim(gated, begin, L_DEV, 0)
        o_s = lax.dynamic_slice_in_dim(grad_out, begin, L_DEV, 0)
        bc_term = jnp.dot(h_s.T, hi_s, preferred_element_type=jnp.float32) + jnp.dot(h_s.T, lo_s, preferred_element_type=jnp.float32)
        return (sums[0] + rounded(jnp.dot(h_s.T, zx_s, preferred_element_type=jnp.float32)), sums[1] + rounded(jnp.dot(h_s.T, dt_s, preferred_element_type=jnp.float32)), sums[2] + rounded(bc_term), sums[3] + rounded(jnp.dot(g_s.T, o_s, preferred_element_type=jnp.float32)))
    start = (jnp.zeros((D, 2 * wide), jnp.float32), jnp.zeros((D, HEADS), jnp.float32), jnp.zeros((D, 2 * STATE), jnp.float32), jnp.zeros((wide, D), jnp.float32))
    grad_wzx, grad_wdt, grad_wbc, grad_wout = lax.fori_loop(0, N_SEQ, accumulate, start)
    return (layer_out, grad_hidden, grad_wzx.reshape(D, 2, wide), grad_wdt, grad_wbc.reshape(D, 2, STATE), grad_dtbias, grad_alog, grad_dskip, grad_gain, grad_wout)
```

```python
import jax
import jax.numpy as jnp
from jax import lax
from jax.sharding import PartitionSpec as P

HEADS = 48
HDIM = 64
BLOCK = 128


EPS_NORM = 1e-05
HIGH = lax.Precision.HIGHEST
MID = lax.Precision.HIGH


def entering(x, axis, combine, identity):
    peers, here = (lax.axis_size(axis), lax.axis_index(axis))
    everything = jax.tree.map(
        lambda part, kind: lax.all_gather(part.astype(kind), axis), x, (jnp.bfloat16, jnp.bfloat16)
    )
    start = jax.tree.map(
        lambda part, zero: jnp.broadcast_to(jnp.asarray(zero, part.dtype), part.shape), x, identity
    )

    def entering_lap(k, before):
        reached = k < here
        new = combine(
            before, jax.tree.map(lambda part, own: part[k].astype(own.dtype), everything, x)
        )
        return jax.tree.map(lambda a, b: jnp.where(reached, a, b), new, before)

    return lax.fori_loop(0, peers, entering_lap, start)


def carried_in(x, axis, combine, identity):
    peers, here = (lax.axis_size(axis), lax.axis_index(axis))
    everything = jax.tree.map(
        lambda part, kind: lax.all_gather(part.astype(kind), axis),
        x,
        jax.tree.map(lambda a: jnp.bfloat16 if a.dtype == jnp.float32 else a.dtype, x),
    )
    start = jax.tree.map(
        lambda part, zero: jnp.broadcast_to(jnp.asarray(zero, part.dtype), part.shape), x, identity
    )

    def carried_lap(k, before):
        at = peers - 1 - k
        reached = at > here
        new = combine(
            before, jax.tree.map(lambda part, own: part[at].astype(own.dtype), everything, x)
        )
        return jax.tree.map(lambda a, b: jnp.where(reached, a, b), new, before)

    return lax.fori_loop(0, peers, carried_lap, start)


def split_inputs(zx_f, dtr_f, bc_f, dt_bias, a_log):
    rows = dtr_f.shape[0]
    nheads = dtr_f.shape[1]
    width = zx_f.shape[2] // nheads
    z_gate = zx_f[:, 0]
    x_in = jax.nn.silu(zx_f[:, 1]).reshape(rows, nheads, width)
    dt_val = jax.nn.softplus(dtr_f + dt_bias[None])
    log_decay = -dt_val * jnp.exp(a_log)[None]
    return (z_gate, x_in, dt_val, log_decay, bc_f[:, 0], bc_f[:, 1])


def ssd_pass(x_in, dt_val, log_decay, b_in, c_in, d_skip, s_init, with_out):
    rows, nheads, width = x_in.shape
    blocks = rows // BLOCK
    lower = jnp.arange(BLOCK)[:, None] >= jnp.arange(BLOCK)[None, :]
    parts = (
        x_in.reshape(blocks, BLOCK, nheads, width),
        dt_val.reshape(blocks, BLOCK, nheads),
        log_decay.reshape(blocks, BLOCK, nheads),
        b_in.reshape(blocks, BLOCK, -1),
        c_in.reshape(blocks, BLOCK, -1),
    )

    def advance(state, block):
        x_blk, dt_blk, ld_blk, b_blk, c_blk = block
        cumul = jnp.cumsum(ld_blk, axis=0)
        tail = cumul[-1]
        inflow = jnp.exp(tail[None] - cumul) * dt_blk
        fresh = state * jnp.exp(tail)[:, None, None] + jnp.einsum(
            "sh,shp,sn->hpn", inflow, x_blk, b_blk, precision=HIGH
        )
        if not with_out:
            return (fresh, None)
        scores = jnp.dot(c_blk, b_blk.T, precision=HIGH)
        gaps = cumul.T[:, :, None] - cumul.T[:, None, :]
        weights = jnp.exp(jnp.where(lower[None], gaps, -1e30)) * scores[None] * dt_blk.T[:, None, :]
        y_blk = jnp.einsum("hts,shp->thp", weights, x_blk, precision=HIGH)
        y_blk = (
            y_blk
            + jnp.einsum("tn,hpn->thp", c_blk, state, precision=HIGH) * jnp.exp(cumul)[:, :, None]
        )
        y_blk = y_blk + d_skip[None, :, None] * x_blk
        return (fresh, y_blk)

    final, outs = lax.scan(advance, s_init, parts)
    return (outs, final)


def mixer(zx_f, dtr_f, bc_f, dt_bias, a_log, d_skip, s_init):
    z_gate, x_in, dt_val, log_decay, b_in, c_in = split_inputs(zx_f, dtr_f, bc_f, dt_bias, a_log)
    outs, final = ssd_pass(x_in, dt_val, log_decay, b_in, c_in, d_skip, s_init, True)
    return outs.reshape(z_gate.shape[0], -1) * jax.nn.silu(z_gate)


def local_states(zx_f, dtr_f, bc_f, dt_bias, a_log):
    z_gate, x_in, dt_val, log_decay, b_in, c_in = split_inputs(zx_f, dtr_f, bc_f, dt_bias, a_log)
    start_state = jnp.zeros((x_in.shape[1], x_in.shape[2], b_in.shape[1]), x_in.dtype)
    outs, final = ssd_pass(x_in, dt_val, log_decay, b_in, c_in, None, start_state, False)
    return (final, jnp.sum(log_decay, axis=0))


def combine(earlier, later):
    return (earlier[0] * later[0], later[0][:, None, None] * earlier[1] + later[1])


def split_pair(value):
    upper = value.astype(jnp.bfloat16)
    lower_part = (value - upper.astype(value.dtype)).astype(jnp.bfloat16)
    return (upper, lower_part)


def input_rows_term(grads, pieces):
    count = pieces[0].shape[0]
    term = jnp.einsum(
        "tc,dc->td", grads[0], pieces[0].reshape(count, -1), preferred_element_type=jnp.float32
    )
    term = term + jnp.einsum("th,dh->td", grads[1], pieces[1], preferred_element_type=jnp.float32)
    flat_bc = pieces[2].reshape(count, -1)
    term = term + jnp.einsum("tc,dc->td", grads[2], flat_bc, preferred_element_type=jnp.float32)
    return term + jnp.einsum("tc,dc->td", grads[3], flat_bc, preferred_element_type=jnp.float32)


def weights_moved(hidden, w_zx, w_dt, w_bc, dt_bias, a_log, d_skip, norm_gain, w_out, grad_out):
    tokens = hidden.shape[0]
    wide = HEADS * HDIM
    local_cols = w_zx.shape[1] * w_zx.shape[2]
    bc_cols = w_bc.shape[1] * w_bc.shape[2]
    head_cols = w_dt.shape[1]
    full_in = lax.all_gather(hidden, "head", axis=1, tiled=True)
    pieces = (
        lax.all_gather(w_zx, "seq", axis=0, tiled=True),
        lax.all_gather(w_dt, "seq", axis=0, tiled=True),
        lax.all_gather(w_bc, "seq", axis=0, tiled=True),
    )
    count = pieces[0].shape[0]
    cols = full_in
    zx_acc = jnp.dot(cols, pieces[0].reshape(count, local_cols), preferred_element_type=jnp.float32)
    dt_acc = jnp.dot(cols, pieces[1], preferred_element_type=jnp.float32)
    bc_acc = jnp.dot(cols, pieces[2].reshape(count, bc_cols), preferred_element_type=jnp.float32)
    zx_b, dtr_b, bc_b = lax.optimization_barrier(
        (zx_acc.astype(jnp.bfloat16), dt_acc.astype(jnp.bfloat16), bc_acc.astype(jnp.bfloat16))
    )
    zx_f = zx_b.astype(jnp.float32).reshape(tokens, 2, -1)
    dtr_f = dtr_b.astype(jnp.float32)
    bc_f = bc_b.astype(jnp.float32).reshape(tokens, 2, -1)
    (s_local, log_total), pull_states = jax.vjp(local_states, zx_f, dtr_f, bc_f, dt_bias, a_log)
    decay = jnp.exp(log_total)
    identity = (jnp.ones_like(decay), jnp.zeros_like(s_local))
    s_in = entering((decay, s_local), "seq", combine, identity)[1]
    mixed, pull_mixer = jax.vjp(mixer, zx_f, dtr_f, bc_f, dt_bias, a_log, d_skip, s_in)
    squares = lax.psum(jnp.sum(mixed * mixed, axis=1), "head")
    rinv = lax.rsqrt(squares / wide + EPS_NORM)
    gated = (mixed * rinv[:, None] * norm_gain[None]).astype(jnp.bfloat16)
    partial_value = jnp.dot(
        gated, lax.all_gather(w_out, "seq", axis=1, tiled=True), preferred_element_type=jnp.float32
    )
    layer_out = lax.psum_scatter(
        partial_value.astype(jnp.bfloat16), "head", scatter_dimension=1, tiled=True
    )
    full_grad = lax.all_gather(grad_out, "head", axis=1, tiled=True)
    piece = lax.all_gather(w_out, "seq", axis=1, tiled=True)
    cols = full_grad
    back = jnp.einsum("tr,kr->tk", cols, piece, preferred_element_type=jnp.float32)
    grad_gated = lax.optimization_barrier(back.astype(jnp.bfloat16))
    out_term = jnp.einsum("tk,td->kd", gated, full_grad, preferred_element_type=jnp.float32)
    grad_wout = lax.psum_scatter(
        out_term.astype(jnp.bfloat16), "seq", scatter_dimension=1, tiled=True
    ).astype(jnp.float32)
    upstream = grad_gated.astype(jnp.float32)
    gain_part = jnp.sum(upstream * mixed * rinv[:, None], axis=0)
    inner = lax.psum(jnp.sum(upstream * norm_gain[None] * mixed, axis=1), "head")
    grad_mixed = (
        rinv[:, None] * norm_gain[None] * upstream
        - mixed * (rinv * rinv * rinv * inner / wide)[:, None]
    )
    first = pull_mixer(grad_mixed)
    ds_in = first[6]
    carried = carried_in((decay, ds_in), "seq", combine, identity)[1]
    grad_log = decay * jnp.sum(carried * s_in, axis=(1, 2))
    second = pull_states((carried, grad_log))
    d_zx = (first[0] + second[0]).reshape(tokens, -1).astype(jnp.bfloat16)
    d_dtr = (first[1] + second[1]).astype(jnp.bfloat16)
    d_bc = (first[2] + second[2]).reshape(tokens, -1)
    bc_upper, bc_lower = split_pair(d_bc)
    grad_dtbias, grad_alog, grad_dskip, grad_gain = lax.psum(
        (first[3] + second[3], first[4] + second[4], first[5], gain_part), "seq"
    )
    term = input_rows_term(
        (d_zx, d_dtr, bc_upper, bc_lower),
        lax.all_gather((w_zx, w_dt, w_bc), "seq", axis=0, tiled=True),
    )
    grad_hidden = lax.psum_scatter(
        term.astype(jnp.bfloat16), "head", scatter_dimension=1, tiled=True
    )
    bc_total = lax.psum(d_bc.astype(jnp.bfloat16), "head").astype(jnp.float32)
    total_upper, total_lower = split_pair(bc_total)
    cols = full_in
    bc_term = jnp.einsum(
        "tr,tc->rc", cols, total_upper, preferred_element_type=jnp.float32
    ) + jnp.einsum("tr,tc->rc", cols, total_lower, preferred_element_type=jnp.float32)
    sums = lax.psum_scatter(
        jnp.concatenate(
            [
                jnp.einsum("tr,tc->rc", cols, d_zx, preferred_element_type=jnp.float32),
                jnp.einsum("tr,th->rh", cols, d_dtr, preferred_element_type=jnp.float32),
                bc_term,
            ],
            axis=1,
        ).astype(jnp.bfloat16),
        "seq",
        scatter_dimension=0,
        tiled=True,
    ).astype(jnp.float32)
    rows_here = w_zx.shape[0]
    grad_wzx = sums[:, :local_cols].reshape(rows_here, 2, -1)
    grad_wdt = sums[:, local_cols : local_cols + head_cols]
    grad_wbc = sums[:, local_cols + head_cols :].reshape(rows_here, 2, -1)
    return (
        layer_out,
        grad_hidden,
        grad_wzx,
        grad_wdt,
        grad_wbc,
        grad_dtbias,
        grad_alog,
        grad_dskip,
        grad_gain,
        grad_wout,
    )


def mixer_cols(z_t, xr_t, dtr_t, b_in, c_in, dt_bias, a_log, d_skip):
    nheads, rows = dtr_t.shape
    blocks = rows // BLOCK
    width = xr_t.shape[0] // nheads
    pos = jnp.arange(BLOCK)
    lower = pos[:, None] >= pos[None, :]
    x = jax.nn.silu(xr_t).reshape(nheads, width, blocks, BLOCK)
    dt = jax.nn.softplus(dtr_t + dt_bias[:, None])
    ld = (-dt * jnp.exp(a_log)[:, None]).reshape(nheads, blocks, BLOCK)
    dt = dt.reshape(nheads, blocks, BLOCK)
    cumul = jnp.einsum("hks,ts->hkt", ld, lower.astype(jnp.float32), precision=HIGH)
    tail = cumul[:, :, -1]
    b_blk = b_in.reshape(blocks, BLOCK, -1)
    c_blk = c_in.reshape(blocks, BLOCK, -1)
    scores = jnp.einsum("ktn,ksn->kts", c_blk, b_blk, precision=MID)
    gaps = cumul[:, :, :, None] - cumul[:, :, None, :]
    weights = jnp.exp(jnp.where(lower, gaps, -1e30)) * scores[None] * dt[:, :, None, :]
    y = jnp.einsum("hkts,hpks->hpkt", weights, x, precision=MID)
    inflow = jnp.exp(tail[:, :, None] - cumul) * dt
    fresh = jnp.einsum("hpks,ksn->hkpn", x * inflow[:, None], b_blk, precision=MID)
    at = jnp.arange(blocks)
    reach = (at[:, None] > at[None, :]).astype(jnp.float32)
    ahead = jnp.einsum("hj,kj->hk", tail, reach, precision=HIGH)
    span = ahead[:, :, None] - (ahead + tail)[:, None, :]
    carry = jnp.exp(jnp.where(at[:, None] > at[None, :], span, -1e30))
    state = jnp.einsum("hkj,hjpn->hkpn", carry, fresh, precision=HIGH)
    y = y + jnp.einsum("ktn,hkpn->hpkt", c_blk, state, precision=MID) * jnp.exp(cumul)[:, None]
    y = y + d_skip[:, None, None, None] * x
    return y.reshape(nheads * width, rows) * jax.nn.silu(z_t)


def activations_moved(hidden, w_zx, w_dt, w_bc, dt_bias, a_log, d_skip, norm_gain, w_out, grad_out):
    f32, bf16 = jnp.float32, jnp.bfloat16
    peers = lax.axis_size("seq")
    s, h = lax.axis_index("seq"), lax.axis_index("head")
    tokens = hidden.shape[0]
    wide = HEADS * HDIM
    heads = w_dt.shape[1] // peers
    span = heads * HDIM
    swap = [(a * peers + b, b * peers + a) for a in range(peers) for b in range(peers)]

    def turned(x):
        return lax.ppermute(x, ("seq", "head"), swap)

    def mine(x, size):
        return lax.dynamic_slice_in_dim(x, s * size, size, 0)

    hid = lax.all_gather(turned(hidden), "head", axis=0, tiled=True)
    gout = lax.all_gather(turned(grad_out), "head", axis=0, tiled=True)
    w_z, w_x = w_zx[:, 0], w_zx[:, 1]
    w_b = w_bc.reshape(w_bc.shape[0], -1)

    def scattered(w):
        part = jnp.einsum("dc,td->ct", w, hid, preferred_element_type=f32).astype(bf16)
        return lax.psum_scatter(part, "seq", scatter_dimension=0, tiled=True)

    xr_b = scattered(w_x)
    hid_h = lax.dynamic_slice_in_dim(hid, h * tokens, tokens, 0)
    bc_part = jnp.dot(hid_h, w_b, preferred_element_type=f32)
    dt_part = jnp.einsum("dc,td->ct", w_dt, hid, preferred_element_type=f32)
    bc_h, dtr_all = lax.psum((bc_part, dt_part), "seq")
    bc_b = lax.all_gather(bc_h.astype(bf16), "head", axis=0, tiled=True)
    z_b = scattered(w_z)
    up_part = jnp.einsum("kd,td->kt", w_out, gout, preferred_element_type=f32).astype(bf16)
    up_b = lax.psum_scatter(up_part, "seq", scatter_dimension=0, tiled=True)
    dtr_b = mine(dtr_all, heads).astype(bf16)
    z_b, xr_b, dtr_b, bc_b, up_b = lax.optimization_barrier((z_b, xr_b, dtr_b, bc_b, up_b))
    states = w_bc.shape[2]
    bc_f = bc_b.astype(f32)
    bias, alog, skip = mine(dt_bias, heads), mine(a_log, heads), mine(d_skip, heads)
    gain = mine(norm_gain, span)[:, None]
    upstream = up_b.astype(f32)
    mixed, pull = jax.vjp(
        mixer_cols, z_b.astype(f32), xr_b.astype(f32), dtr_b.astype(f32),
        bc_f[:, :states], bc_f[:, states:], bias, alog, skip,
    )
    sums = jnp.stack([jnp.sum(mixed * mixed, axis=0), jnp.sum(upstream * gain * mixed, axis=0)])
    squares, inner = lax.psum(sums, ("seq", "head"))
    rinv = lax.rsqrt(squares / wide + EPS_NORM)
    gated = (mixed * rinv[None] * gain).astype(bf16)
    gated_all = lax.all_gather(gated, "seq", axis=0, tiled=True)
    grad_mixed = rinv[None] * gain * upstream - mixed * (rinv * rinv * rinv * inner / wide)[None]
    gain_part = jnp.sum(upstream * mixed * rinv[None], axis=1)
    d_z, d_xr, d_dtr, d_b, d_c, g_bias, g_alog, g_skip = pull(grad_mixed)
    dx_all = lax.all_gather(d_xr.astype(bf16), "seq", axis=0, tiled=True)
    dz_all = lax.all_gather(d_z.astype(bf16), "seq", axis=0, tiled=True)
    d_bc = lax.psum(jnp.concatenate([d_b, d_c], axis=1).astype(bf16), ("seq", "head")).astype(f32)
    small = jnp.concatenate([g_bias, g_alog, g_skip, gain_part])
    small_all, ddt_all = lax.all_gather((small, d_dtr.astype(bf16)), "seq", axis=0)
    ddt_all = ddt_all.reshape(peers * heads, -1)
    grad_dtbias, grad_alog, grad_dskip = (
        small_all[:, i * heads : (i + 1) * heads].reshape(-1) for i in range(3)
    )
    grad_gain = small_all[:, 3 * heads :].reshape(-1)

    out_part = jnp.einsum("kt,kd->td", gated_all, w_out, preferred_element_type=f32)
    layer_out = turned(
        lax.psum_scatter(out_part.astype(bf16), "head", scatter_dimension=0, tiled=True)
    )
    grad_wout = jnp.dot(gated_all, gout, preferred_element_type=f32)

    hid_part = jnp.einsum("ct,dc->td", dx_all, w_x, preferred_element_type=f32)
    hid_part = hid_part + jnp.einsum("ct,dc->td", dz_all, w_z, preferred_element_type=f32)
    hid_part = hid_part + jnp.einsum("ct,dc->td", ddt_all, w_dt, preferred_element_type=f32)
    hid_rows = lax.psum_scatter(hid_part.astype(bf16), "head", scatter_dimension=0, tiled=True)
    upper, lower_part = split_pair(d_bc)
    hid_rows = hid_rows.astype(f32)
    for part in (upper, lower_part):
        rows = lax.dynamic_slice_in_dim(part, h * tokens, tokens, 0)
        hid_rows = hid_rows + jnp.einsum("tc,dc->td", rows, w_b, preferred_element_type=f32)
    grad_hidden = turned(hid_rows.astype(bf16))

    grad_wzx = jnp.stack(
        [jnp.einsum("td,ct->dc", hid, g, preferred_element_type=f32) for g in (dz_all, dx_all)],
        axis=1,
    )
    grad_wdt = jnp.einsum("td,ct->dc", hid, ddt_all, preferred_element_type=f32)
    grad_wbc = jnp.einsum("td,tc->dc", hid, upper, preferred_element_type=f32) + jnp.einsum(
        "td,tc->dc", hid, lower_part, preferred_element_type=f32
    )
    return (
        layer_out,
        grad_hidden,
        grad_wzx,
        grad_wdt,
        grad_wbc.reshape(w_bc.shape),
        grad_dtbias,
        grad_alog,
        grad_dskip,
        grad_gain,
        grad_wout,
    )


def solution(mesh):
    seq, head = mesh.shape["seq"], mesh.shape["head"]
    even = seq == head and HEADS % (seq * head) == 0
    on_device = activations_moved if even else weights_moved
    in_specs = (
        P(("groups", "seq"), "head"),
        P("seq", None, "head"),
        P("seq", "head"),
        P("seq", None, None),
        P("head"),
        P("head"),
        P("head"),
        P("head"),
        P("head", "seq"),
        P(("groups", "seq"), "head"),
    )
    out_specs = (
        P(("groups", "seq"), "head"),
        P(("groups", "seq"), "head"),
        P(("groups", "seq"), None, "head"),
        P(("groups", "seq"), "head"),
        P(("groups", "seq"), None, None),
        P(("groups", "head")),
        P(("groups", "head")),
        P(("groups", "head")),
        P(("groups", "head")),
        P(("groups", "head"), "seq"),
    )
    return jax.shard_map(
        on_device, mesh=mesh, in_specs=in_specs, out_specs=out_specs, check_vma=False
    )
```

```python
import jax
import jax.numpy as jnp
from jax import lax
from jax.sharding import PartitionSpec as P

HEADS = 48
HDIM = 64
BLOCK = 128


EPS_NORM = 1e-05
HIGH = lax.Precision.HIGHEST
MID = lax.Precision.HIGH


def entering(x, axis, combine, identity):
    peers, here = (lax.axis_size(axis), lax.axis_index(axis))
    everything = jax.tree.map(
        lambda part, kind: lax.all_gather(part.astype(kind), axis), x, (jnp.bfloat16, jnp.bfloat16)
    )
    start = jax.tree.map(
        lambda part, zero: jnp.broadcast_to(jnp.asarray(zero, part.dtype), part.shape), x, identity
    )

    def entering_lap(k, before):
        reached = k < here
        new = combine(
            before, jax.tree.map(lambda part, own: part[k].astype(own.dtype), everything, x)
        )
        return jax.tree.map(lambda a, b: jnp.where(reached, a, b), new, before)

    return lax.fori_loop(0, peers, entering_lap, start)


def carried_in(x, axis, combine, identity):
    peers, here = (lax.axis_size(axis), lax.axis_index(axis))
    everything = jax.tree.map(
        lambda part, kind: lax.all_gather(part.astype(kind), axis),
        x,
        jax.tree.map(lambda a: jnp.bfloat16 if a.dtype == jnp.float32 else a.dtype, x),
    )
    start = jax.tree.map(
        lambda part, zero: jnp.broadcast_to(jnp.asarray(zero, part.dtype), part.shape), x, identity
    )

    def carried_lap(k, before):
        at = peers - 1 - k
        reached = at > here
        new = combine(
            before, jax.tree.map(lambda part, own: part[at].astype(own.dtype), everything, x)
        )
        return jax.tree.map(lambda a, b: jnp.where(reached, a, b), new, before)

    return lax.fori_loop(0, peers, carried_lap, start)


def split_inputs(zx_f, dtr_f, bc_f, dt_bias, a_log):
    rows = dtr_f.shape[0]
    nheads = dtr_f.shape[1]
    width = zx_f.shape[2] // nheads
    z_gate = zx_f[:, 0]
    x_in = jax.nn.silu(zx_f[:, 1]).reshape(rows, nheads, width)
    dt_val = jax.nn.softplus(dtr_f + dt_bias[None])
    log_decay = -dt_val * jnp.exp(a_log)[None]
    return (z_gate, x_in, dt_val, log_decay, bc_f[:, 0], bc_f[:, 1])


def ssd_pass(x_in, dt_val, log_decay, b_in, c_in, d_skip, s_init, with_out):
    rows, nheads, width = x_in.shape
    blocks = rows // BLOCK
    lower = jnp.arange(BLOCK)[:, None] >= jnp.arange(BLOCK)[None, :]
    parts = (
        x_in.reshape(blocks, BLOCK, nheads, width),
        dt_val.reshape(blocks, BLOCK, nheads),
        log_decay.reshape(blocks, BLOCK, nheads),
        b_in.reshape(blocks, BLOCK, -1),
        c_in.reshape(blocks, BLOCK, -1),
    )

    def advance(state, block):
        x_blk, dt_blk, ld_blk, b_blk, c_blk = block
        cumul = jnp.cumsum(ld_blk, axis=0)
        tail = cumul[-1]
        inflow = jnp.exp(tail[None] - cumul) * dt_blk
        fresh = state * jnp.exp(tail)[:, None, None] + jnp.einsum(
            "sh,shp,sn->hpn", inflow, x_blk, b_blk, precision=HIGH
        )
        if not with_out:
            return (fresh, None)
        scores = jnp.dot(c_blk, b_blk.T, precision=HIGH)
        gaps = cumul.T[:, :, None] - cumul.T[:, None, :]
        weights = jnp.exp(jnp.where(lower[None], gaps, -1e30)) * scores[None] * dt_blk.T[:, None, :]
        y_blk = jnp.einsum("hts,shp->thp", weights, x_blk, precision=HIGH)
        y_blk = (
            y_blk
            + jnp.einsum("tn,hpn->thp", c_blk, state, precision=HIGH) * jnp.exp(cumul)[:, :, None]
        )
        y_blk = y_blk + d_skip[None, :, None] * x_blk
        return (fresh, y_blk)

    final, outs = lax.scan(advance, s_init, parts)
    return (outs, final)


def mixer(zx_f, dtr_f, bc_f, dt_bias, a_log, d_skip, s_init):
    z_gate, x_in, dt_val, log_decay, b_in, c_in = split_inputs(zx_f, dtr_f, bc_f, dt_bias, a_log)
    outs, final = ssd_pass(x_in, dt_val, log_decay, b_in, c_in, d_skip, s_init, True)
    return outs.reshape(z_gate.shape[0], -1) * jax.nn.silu(z_gate)


def local_states(zx_f, dtr_f, bc_f, dt_bias, a_log):
    z_gate, x_in, dt_val, log_decay, b_in, c_in = split_inputs(zx_f, dtr_f, bc_f, dt_bias, a_log)
    start_state = jnp.zeros((x_in.shape[1], x_in.shape[2], b_in.shape[1]), x_in.dtype)
    outs, final = ssd_pass(x_in, dt_val, log_decay, b_in, c_in, None, start_state, False)
    return (final, jnp.sum(log_decay, axis=0))


def combine(earlier, later):
    return (earlier[0] * later[0], later[0][:, None, None] * earlier[1] + later[1])


def split_pair(value):
    upper = value.astype(jnp.bfloat16)
    lower_part = (value - upper.astype(value.dtype)).astype(jnp.bfloat16)
    return (upper, lower_part)


def input_rows_term(grads, pieces):
    count = pieces[0].shape[0]
    term = jnp.einsum(
        "tc,dc->td", grads[0], pieces[0].reshape(count, -1), preferred_element_type=jnp.float32
    )
    term = term + jnp.einsum("th,dh->td", grads[1], pieces[1], preferred_element_type=jnp.float32)
    flat_bc = pieces[2].reshape(count, -1)
    term = term + jnp.einsum("tc,dc->td", grads[2], flat_bc, preferred_element_type=jnp.float32)
    return term + jnp.einsum("tc,dc->td", grads[3], flat_bc, preferred_element_type=jnp.float32)


def weights_moved(hidden, w_zx, w_dt, w_bc, dt_bias, a_log, d_skip, norm_gain, w_out, grad_out):
    tokens = hidden.shape[0]
    wide = HEADS * HDIM
    local_cols = w_zx.shape[1] * w_zx.shape[2]
    bc_cols = w_bc.shape[1] * w_bc.shape[2]
    head_cols = w_dt.shape[1]
    full_in = lax.all_gather(hidden, "head", axis=1, tiled=True)
    pieces = (
        lax.all_gather(w_zx, "seq", axis=0, tiled=True),
        lax.all_gather(w_dt, "seq", axis=0, tiled=True),
        lax.all_gather(w_bc, "seq", axis=0, tiled=True),
    )
    count = pieces[0].shape[0]
    cols = full_in
    zx_acc = jnp.dot(cols, pieces[0].reshape(count, local_cols), preferred_element_type=jnp.float32)
    dt_acc = jnp.dot(cols, pieces[1], preferred_element_type=jnp.float32)
    bc_acc = jnp.dot(cols, pieces[2].reshape(count, bc_cols), preferred_element_type=jnp.float32)
    zx_b, dtr_b, bc_b = lax.optimization_barrier(
        (zx_acc.astype(jnp.bfloat16), dt_acc.astype(jnp.bfloat16), bc_acc.astype(jnp.bfloat16))
    )
    zx_f = zx_b.astype(jnp.float32).reshape(tokens, 2, -1)
    dtr_f = dtr_b.astype(jnp.float32)
    bc_f = bc_b.astype(jnp.float32).reshape(tokens, 2, -1)
    (s_local, log_total), pull_states = jax.vjp(local_states, zx_f, dtr_f, bc_f, dt_bias, a_log)
    decay = jnp.exp(log_total)
    identity = (jnp.ones_like(decay), jnp.zeros_like(s_local))
    s_in = entering((decay, s_local), "seq", combine, identity)[1]
    mixed, pull_mixer = jax.vjp(mixer, zx_f, dtr_f, bc_f, dt_bias, a_log, d_skip, s_in)
    squares = lax.psum(jnp.sum(mixed * mixed, axis=1), "head")
    rinv = lax.rsqrt(squares / wide + EPS_NORM)
    gated = (mixed * rinv[:, None] * norm_gain[None]).astype(jnp.bfloat16)
    partial_value = jnp.dot(
        gated, lax.all_gather(w_out, "seq", axis=1, tiled=True), preferred_element_type=jnp.float32
    )
    layer_out = lax.psum_scatter(
        partial_value.astype(jnp.bfloat16), "head", scatter_dimension=1, tiled=True
    )
    full_grad = lax.all_gather(grad_out, "head", axis=1, tiled=True)
    piece = lax.all_gather(w_out, "seq", axis=1, tiled=True)
    cols = full_grad
    back = jnp.einsum("tr,kr->tk", cols, piece, preferred_element_type=jnp.float32)
    grad_gated = lax.optimization_barrier(back.astype(jnp.bfloat16))
    out_term = jnp.einsum("tk,td->kd", gated, full_grad, preferred_element_type=jnp.float32)
    grad_wout = lax.psum_scatter(
        out_term.astype(jnp.bfloat16), "seq", scatter_dimension=1, tiled=True
    ).astype(jnp.float32)
    upstream = grad_gated.astype(jnp.float32)
    gain_part = jnp.sum(upstream * mixed * rinv[:, None], axis=0)
    inner = lax.psum(jnp.sum(upstream * norm_gain[None] * mixed, axis=1), "head")
    grad_mixed = (
        rinv[:, None] * norm_gain[None] * upstream
        - mixed * (rinv * rinv * rinv * inner / wide)[:, None]
    )
    first = pull_mixer(grad_mixed)
    ds_in = first[6]
    carried = carried_in((decay, ds_in), "seq", combine, identity)[1]
    grad_log = decay * jnp.sum(carried * s_in, axis=(1, 2))
    second = pull_states((carried, grad_log))
    d_zx = (first[0] + second[0]).reshape(tokens, -1).astype(jnp.bfloat16)
    d_dtr = (first[1] + second[1]).astype(jnp.bfloat16)
    d_bc = (first[2] + second[2]).reshape(tokens, -1)
    bc_upper, bc_lower = split_pair(d_bc)
    grad_dtbias, grad_alog, grad_dskip, grad_gain = lax.psum(
        (first[3] + second[3], first[4] + second[4], first[5], gain_part), "seq"
    )
    term = input_rows_term(
        (d_zx, d_dtr, bc_upper, bc_lower),
        lax.all_gather((w_zx, w_dt, w_bc), "seq", axis=0, tiled=True),
    )
    grad_hidden = lax.psum_scatter(
        term.astype(jnp.bfloat16), "head", scatter_dimension=1, tiled=True
    )
    bc_total = lax.psum(d_bc.astype(jnp.bfloat16), "head").astype(jnp.float32)
    total_upper, total_lower = split_pair(bc_total)
    cols = full_in
    bc_term = jnp.einsum(
        "tr,tc->rc", cols, total_upper, preferred_element_type=jnp.float32
    ) + jnp.einsum("tr,tc->rc", cols, total_lower, preferred_element_type=jnp.float32)
    sums = lax.psum_scatter(
        jnp.concatenate(
            [
                jnp.einsum("tr,tc->rc", cols, d_zx, preferred_element_type=jnp.float32),
                jnp.einsum("tr,th->rh", cols, d_dtr, preferred_element_type=jnp.float32),
                bc_term,
            ],
            axis=1,
        ).astype(jnp.bfloat16),
        "seq",
        scatter_dimension=0,
        tiled=True,
    ).astype(jnp.float32)
    rows_here = w_zx.shape[0]
    grad_wzx = sums[:, :local_cols].reshape(rows_here, 2, -1)
    grad_wdt = sums[:, local_cols : local_cols + head_cols]
    grad_wbc = sums[:, local_cols + head_cols :].reshape(rows_here, 2, -1)
    return (
        layer_out,
        grad_hidden,
        grad_wzx,
        grad_wdt,
        grad_wbc,
        grad_dtbias,
        grad_alog,
        grad_dskip,
        grad_gain,
        grad_wout,
    )


def mixer_cols(z_t, xr_t, dtr_t, b_t, c_t, dt_bias, a_log, d_skip):
    nheads, rows = dtr_t.shape
    blocks = rows // BLOCK
    width = xr_t.shape[0] // nheads
    pos = jnp.arange(BLOCK)
    lower = pos[:, None] >= pos[None, :]
    x = jax.nn.silu(xr_t).reshape(nheads, width, blocks, BLOCK)
    dt = jax.nn.softplus(dtr_t + dt_bias[:, None])
    ld = (-dt * jnp.exp(a_log)[:, None]).reshape(nheads, blocks, BLOCK)
    dt = dt.reshape(nheads, blocks, BLOCK)
    cumul = jnp.einsum("hks,ts->hkt", ld, lower.astype(jnp.float32), precision=HIGH)
    tail = cumul[:, :, -1]
    b_blk = b_t.reshape(-1, blocks, BLOCK)
    c_blk = c_t.reshape(-1, blocks, BLOCK)
    scores = jnp.einsum("nkt,nks->kts", c_blk, b_blk, precision=MID)
    gaps = cumul[:, :, :, None] - cumul[:, :, None, :]
    weights = jnp.exp(jnp.where(lower, gaps, -1e30)) * scores[None] * dt[:, :, None, :]
    y = jnp.einsum("hkts,hpks->hpkt", weights, x, precision=MID)
    inflow = jnp.exp(tail[:, :, None] - cumul) * dt
    fresh = jnp.einsum("hpks,nks->hkpn", x * inflow[:, None], b_blk, precision=MID)
    at = jnp.arange(blocks)
    reach = (at[:, None] > at[None, :]).astype(jnp.float32)
    ahead = jnp.einsum("hj,kj->hk", tail, reach, precision=HIGH)
    span = ahead[:, :, None] - (ahead + tail)[:, None, :]
    carry = jnp.exp(jnp.where(at[:, None] > at[None, :], span, -1e30))
    state = jnp.einsum("hkj,hjpn->hkpn", carry, fresh, precision=HIGH)
    y = y + jnp.einsum("nkt,hkpn->hpkt", c_blk, state, precision=MID) * jnp.exp(cumul)[:, None]
    y = y + d_skip[:, None, None, None] * x
    return y.reshape(nheads * width, rows) * jax.nn.silu(z_t)


def shifted(x, k):
    count = lax.axis_size("head")
    return lax.ppermute(x, "head", [(i, (i + k) % count) for i in range(count)])


def head_gather(x):
    count, h = lax.axis_size("head"), lax.axis_index("head")
    rows = x.shape[0]
    whole = jnp.zeros((count * rows,) + x.shape[1:], x.dtype)
    for k in range(count):
        part = shifted(x, k) if k else x
        whole = lax.dynamic_update_slice_in_dim(whole, part, lax.rem(h + count - k, count) * rows, 0)
    return whole


def head_sum(x, axis):
    count, h = lax.axis_size("head"), lax.axis_index("head")
    size = x.shape[axis] // count
    total = None
    for k in range(count):
        part = lax.dynamic_slice_in_dim(x, lax.rem(h + k, count) * size, size, axis)
        part = (shifted(part, k) if k else part).astype(jnp.float32)
        total = part if total is None else total + part
    return total


def activations_moved(hidden, w_zx, w_dt, w_bc, dt_bias, a_log, d_skip, norm_gain, w_out, grad_out):
    f32, bf16 = jnp.float32, jnp.bfloat16
    peers = lax.axis_size("seq")
    s, h = lax.axis_index("seq"), lax.axis_index("head")
    tokens = hidden.shape[0]
    rows = tokens * peers
    wide = HEADS * HDIM
    heads = w_dt.shape[1] // peers
    span = heads * HDIM
    states = w_bc.shape[2]
    chans = 2 * states // peers
    lines = chans * tokens // rows
    swap = [(a * peers + b, b * peers + a) for a in range(peers) for b in range(peers)]

    def turned(x):
        return lax.ppermute(x, ("seq", "head"), swap)

    def mine(x, size):
        return lax.dynamic_slice_in_dim(x, s * size, size, 0)

    w_z, w_x = w_zx[:, 0], w_zx[:, 1]
    w_b = w_bc.reshape(w_bc.shape[0], -1)
    hid = head_gather(turned(hidden))
    grad_out, hid = lax.optimization_barrier((grad_out, hid))
    gout = head_gather(turned(grad_out))

    def times_hidden(w, cols):
        return jnp.einsum("dc,td->ct", w, cols, preferred_element_type=f32).astype(bf16)

    x_part = times_hidden(w_x, hid).reshape(peers, span, rows)
    hid_h = lax.dynamic_slice_in_dim(hid, h * tokens, tokens, 0)
    bc_part = times_hidden(w_b, hid_h).reshape(peers, lines, rows)
    dt_part = times_hidden(w_dt, hid).reshape(peers, heads, rows)
    dt_part = jnp.pad(dt_part, ((0, 0), (0, -heads % 16), (0, 0)))
    packed = jnp.concatenate([x_part, bc_part, dt_part], axis=1)
    packed, hid = lax.optimization_barrier((packed, hid))
    mixed_in = lax.psum_scatter(packed, "seq", scatter_dimension=0, tiled=True)[0]
    z_b = lax.psum_scatter(times_hidden(w_z, hid), "seq", scatter_dimension=0, tiled=True)
    up_part = jnp.einsum("kd,td->kt", w_out, gout, preferred_element_type=f32).astype(bf16)
    up_b = lax.psum_scatter(up_part, "seq", scatter_dimension=0, tiled=True)
    xr_b = mixed_in[:span]
    dtr_b = mixed_in[span + lines : span + lines + heads]
    bc_b = lax.all_gather(
        mixed_in[span : span + lines].reshape(chans, tokens), ("seq", "head"), axis=0
    )
    bc_b = bc_b.reshape(peers, -1, chans, tokens).transpose(0, 2, 1, 3).reshape(2, states, rows)
    bc_f = bc_b.astype(f32)
    bias, alog, skip = mine(dt_bias, heads), mine(a_log, heads), mine(d_skip, heads)
    gain = mine(norm_gain, span)[:, None]
    upstream = up_b.astype(f32)
    mixed, pull = jax.vjp(
        mixer_cols, z_b.astype(f32), xr_b.astype(f32), dtr_b.astype(f32),
        bc_f[0], bc_f[1], bias, alog, skip,
    )
    sums = jnp.stack([jnp.sum(mixed * mixed, axis=0), jnp.sum(upstream * gain * mixed, axis=0)])
    squares, inner = lax.psum(lax.psum(sums, "head"), "seq")
    rinv = lax.rsqrt(squares / wide + EPS_NORM)
    gated = (mixed * rinv[None] * gain).astype(bf16)
    gated_all = lax.all_gather(gated, "seq", axis=0, tiled=True)
    grad_mixed = rinv[None] * gain * upstream - mixed * (rinv * rinv * rinv * inner / wide)[None]
    gain_part = jnp.sum(upstream * mixed * rinv[None], axis=1)
    d_z, d_xr, d_dtr, d_b, d_c, g_bias, g_alog, g_skip = pull(grad_mixed)
    dz_all = lax.all_gather(d_z.astype(bf16), "seq", axis=0, tiled=True)
    d_bc_h = head_sum(jnp.concatenate([d_b, d_c], axis=0).astype(bf16), 1)
    small = jnp.concatenate([g_bias, g_alog, g_skip, gain_part])
    fill = -small.shape[0] % rows
    small = jnp.pad(small, (0, fill)).reshape(-1, rows)
    misc = jnp.concatenate([d_dtr.astype(bf16), *split_pair(small)], axis=0)
    misc = jnp.pad(misc, ((0, -misc.shape[0] % 16), (0, 0)))
    wave = jnp.concatenate(
        [d_xr.astype(bf16), d_bc_h.astype(bf16).reshape(-1, rows), misc], axis=0
    )
    waves = lax.all_gather(wave, "seq", axis=0)
    dx_all = waves[:, :span].reshape(peers * span, rows)
    d_bc = jnp.sum(waves[:, span : span + peers * lines].astype(f32), axis=0)
    d_bc = d_bc.reshape(2 * states, tokens)
    rest = waves[:, span + peers * lines :]
    ddt_all = rest[:, :heads].reshape(peers * heads, rows)
    count = small.shape[0]
    pair = rest[:, heads : heads + 2 * count].astype(f32)
    small_all = (pair[:, :count] + pair[:, count:]).reshape(peers, -1)
    grad_dtbias, grad_alog, grad_dskip = (
        small_all[:, i * heads : (i + 1) * heads].reshape(-1) for i in range(3)
    )
    grad_gain = small_all[:, 3 * heads : 3 * heads + span].reshape(-1)

    out_part = jnp.einsum("kt,kd->td", gated_all, w_out, preferred_element_type=f32)
    layer_out = turned(head_sum(out_part.astype(bf16), 0).astype(bf16))
    grad_wout = jnp.dot(gated_all, gout, preferred_element_type=f32)

    hid_part = jnp.einsum("ct,dc->td", dz_all, w_z, preferred_element_type=f32)
    hid_part = hid_part + jnp.einsum("ct,dc->td", dx_all, w_x, preferred_element_type=f32)
    hid_part = hid_part + jnp.einsum("ct,dc->td", ddt_all, w_dt, preferred_element_type=f32)
    hid_rows = head_sum(hid_part.astype(bf16), 0)
    for part in split_pair(d_bc):
        hid_rows = hid_rows + jnp.einsum("ct,dc->td", part, w_b, preferred_element_type=f32)
    grad_hidden = turned(hid_rows.astype(bf16))

    grad_wzx = jnp.stack(
        [jnp.einsum("td,ct->dc", hid, g, preferred_element_type=f32) for g in (dz_all, dx_all)],
        axis=1,
    )
    grad_wdt = jnp.einsum("td,ct->dc", hid, ddt_all, preferred_element_type=f32)
    bc_all = lax.all_gather(d_bc.astype(bf16), "head", axis=1, tiled=True)
    grad_wbc = jnp.einsum("td,ct->dc", hid, bc_all, preferred_element_type=f32)
    return (
        layer_out,
        grad_hidden,
        grad_wzx,
        grad_wdt,
        grad_wbc.reshape(w_bc.shape),
        grad_dtbias,
        grad_alog,
        grad_dskip,
        grad_gain,
        grad_wout,
    )


def solution(mesh):
    seq, head = mesh.shape["seq"], mesh.shape["head"]
    even = seq == head and HEADS % (seq * head) == 0
    on_device = activations_moved if even else weights_moved
    in_specs = (
        P(("groups", "seq"), "head"),
        P("seq", None, "head"),
        P("seq", "head"),
        P("seq", None, None),
        P("head"),
        P("head"),
        P("head"),
        P("head"),
        P("head", "seq"),
        P(("groups", "seq"), "head"),
    )
    out_specs = (
        P(("groups", "seq"), "head"),
        P(("groups", "seq"), "head"),
        P(("groups", "seq"), None, "head"),
        P(("groups", "seq"), "head"),
        P(("groups", "seq"), None, None),
        P(("groups", "head")),
        P(("groups", "head")),
        P(("groups", "head")),
        P(("groups", "head")),
        P(("groups", "head"), "seq"),
    )
    return jax.shard_map(
        on_device, mesh=mesh, in_specs=in_specs, out_specs=out_specs, check_vma=False
    )
```

```python
import jax
import jax.numpy as jnp
from jax import lax
from jax.sharding import PartitionSpec as P

HEADS = 48
HDIM = 64
BLOCK = 128


EPS_NORM = 1e-05
HIGH = lax.Precision.HIGHEST
MID = lax.Precision.HIGH


def entering(x, axis, combine, identity):
    peers, here = (lax.axis_size(axis), lax.axis_index(axis))
    everything = jax.tree.map(
        lambda part, kind: lax.all_gather(part.astype(kind), axis), x, (jnp.bfloat16, jnp.bfloat16)
    )
    start = jax.tree.map(
        lambda part, zero: jnp.broadcast_to(jnp.asarray(zero, part.dtype), part.shape), x, identity
    )

    def entering_lap(k, before):
        reached = k < here
        new = combine(
            before, jax.tree.map(lambda part, own: part[k].astype(own.dtype), everything, x)
        )
        return jax.tree.map(lambda a, b: jnp.where(reached, a, b), new, before)

    return lax.fori_loop(0, peers, entering_lap, start)


def carried_in(x, axis, combine, identity):
    peers, here = (lax.axis_size(axis), lax.axis_index(axis))
    everything = jax.tree.map(
        lambda part, kind: lax.all_gather(part.astype(kind), axis),
        x,
        jax.tree.map(lambda a: jnp.bfloat16 if a.dtype == jnp.float32 else a.dtype, x),
    )
    start = jax.tree.map(
        lambda part, zero: jnp.broadcast_to(jnp.asarray(zero, part.dtype), part.shape), x, identity
    )

    def carried_lap(k, before):
        at = peers - 1 - k
        reached = at > here
        new = combine(
            before, jax.tree.map(lambda part, own: part[at].astype(own.dtype), everything, x)
        )
        return jax.tree.map(lambda a, b: jnp.where(reached, a, b), new, before)

    return lax.fori_loop(0, peers, carried_lap, start)


def split_inputs(zx_f, dtr_f, bc_f, dt_bias, a_log):
    rows = dtr_f.shape[0]
    nheads = dtr_f.shape[1]
    width = zx_f.shape[2] // nheads
    z_gate = zx_f[:, 0]
    x_in = jax.nn.silu(zx_f[:, 1]).reshape(rows, nheads, width)
    dt_val = jax.nn.softplus(dtr_f + dt_bias[None])
    log_decay = -dt_val * jnp.exp(a_log)[None]
    return (z_gate, x_in, dt_val, log_decay, bc_f[:, 0], bc_f[:, 1])


def ssd_pass(x_in, dt_val, log_decay, b_in, c_in, d_skip, s_init, with_out):
    rows, nheads, width = x_in.shape
    blocks = rows // BLOCK
    lower = jnp.arange(BLOCK)[:, None] >= jnp.arange(BLOCK)[None, :]
    parts = (
        x_in.reshape(blocks, BLOCK, nheads, width),
        dt_val.reshape(blocks, BLOCK, nheads),
        log_decay.reshape(blocks, BLOCK, nheads),
        b_in.reshape(blocks, BLOCK, -1),
        c_in.reshape(blocks, BLOCK, -1),
    )

    def advance(state, block):
        x_blk, dt_blk, ld_blk, b_blk, c_blk = block
        cumul = jnp.cumsum(ld_blk, axis=0)
        tail = cumul[-1]
        inflow = jnp.exp(tail[None] - cumul) * dt_blk
        fresh = state * jnp.exp(tail)[:, None, None] + jnp.einsum(
            "sh,shp,sn->hpn", inflow, x_blk, b_blk, precision=HIGH
        )
        if not with_out:
            return (fresh, None)
        scores = jnp.dot(c_blk, b_blk.T, precision=HIGH)
        gaps = cumul.T[:, :, None] - cumul.T[:, None, :]
        weights = jnp.exp(jnp.where(lower[None], gaps, -1e30)) * scores[None] * dt_blk.T[:, None, :]
        y_blk = jnp.einsum("hts,shp->thp", weights, x_blk, precision=HIGH)
        y_blk = (
            y_blk
            + jnp.einsum("tn,hpn->thp", c_blk, state, precision=HIGH) * jnp.exp(cumul)[:, :, None]
        )
        y_blk = y_blk + d_skip[None, :, None] * x_blk
        return (fresh, y_blk)

    final, outs = lax.scan(advance, s_init, parts)
    return (outs, final)


def mixer(zx_f, dtr_f, bc_f, dt_bias, a_log, d_skip, s_init):
    z_gate, x_in, dt_val, log_decay, b_in, c_in = split_inputs(zx_f, dtr_f, bc_f, dt_bias, a_log)
    outs, final = ssd_pass(x_in, dt_val, log_decay, b_in, c_in, d_skip, s_init, True)
    return outs.reshape(z_gate.shape[0], -1) * jax.nn.silu(z_gate)


def local_states(zx_f, dtr_f, bc_f, dt_bias, a_log):
    z_gate, x_in, dt_val, log_decay, b_in, c_in = split_inputs(zx_f, dtr_f, bc_f, dt_bias, a_log)
    start_state = jnp.zeros((x_in.shape[1], x_in.shape[2], b_in.shape[1]), x_in.dtype)
    outs, final = ssd_pass(x_in, dt_val, log_decay, b_in, c_in, None, start_state, False)
    return (final, jnp.sum(log_decay, axis=0))


def combine(earlier, later):
    return (earlier[0] * later[0], later[0][:, None, None] * earlier[1] + later[1])


def split_pair(value):
    upper = value.astype(jnp.bfloat16)
    lower_part = (value - upper.astype(value.dtype)).astype(jnp.bfloat16)
    return (upper, lower_part)


def input_rows_term(grads, pieces):
    count = pieces[0].shape[0]
    term = jnp.einsum(
        "tc,dc->td", grads[0], pieces[0].reshape(count, -1), preferred_element_type=jnp.float32
    )
    term = term + jnp.einsum("th,dh->td", grads[1], pieces[1], preferred_element_type=jnp.float32)
    flat_bc = pieces[2].reshape(count, -1)
    term = term + jnp.einsum("tc,dc->td", grads[2], flat_bc, preferred_element_type=jnp.float32)
    return term + jnp.einsum("tc,dc->td", grads[3], flat_bc, preferred_element_type=jnp.float32)


def weights_moved(hidden, w_zx, w_dt, w_bc, dt_bias, a_log, d_skip, norm_gain, w_out, grad_out):
    tokens = hidden.shape[0]
    wide = HEADS * HDIM
    local_cols = w_zx.shape[1] * w_zx.shape[2]
    bc_cols = w_bc.shape[1] * w_bc.shape[2]
    head_cols = w_dt.shape[1]
    full_in = lax.all_gather(hidden, "head", axis=1, tiled=True)
    pieces = (
        lax.all_gather(w_zx, "seq", axis=0, tiled=True),
        lax.all_gather(w_dt, "seq", axis=0, tiled=True),
        lax.all_gather(w_bc, "seq", axis=0, tiled=True),
    )
    count = pieces[0].shape[0]
    cols = full_in
    zx_acc = jnp.dot(cols, pieces[0].reshape(count, local_cols), preferred_element_type=jnp.float32)
    dt_acc = jnp.dot(cols, pieces[1], preferred_element_type=jnp.float32)
    bc_acc = jnp.dot(cols, pieces[2].reshape(count, bc_cols), preferred_element_type=jnp.float32)
    zx_b, dtr_b, bc_b = lax.optimization_barrier(
        (zx_acc.astype(jnp.bfloat16), dt_acc.astype(jnp.bfloat16), bc_acc.astype(jnp.bfloat16))
    )
    zx_f = zx_b.astype(jnp.float32).reshape(tokens, 2, -1)
    dtr_f = dtr_b.astype(jnp.float32)
    bc_f = bc_b.astype(jnp.float32).reshape(tokens, 2, -1)
    (s_local, log_total), pull_states = jax.vjp(local_states, zx_f, dtr_f, bc_f, dt_bias, a_log)
    decay = jnp.exp(log_total)
    identity = (jnp.ones_like(decay), jnp.zeros_like(s_local))
    s_in = entering((decay, s_local), "seq", combine, identity)[1]
    mixed, pull_mixer = jax.vjp(mixer, zx_f, dtr_f, bc_f, dt_bias, a_log, d_skip, s_in)
    squares = lax.psum(jnp.sum(mixed * mixed, axis=1), "head")
    rinv = lax.rsqrt(squares / wide + EPS_NORM)
    gated = (mixed * rinv[:, None] * norm_gain[None]).astype(jnp.bfloat16)
    partial_value = jnp.dot(
        gated, lax.all_gather(w_out, "seq", axis=1, tiled=True), preferred_element_type=jnp.float32
    )
    layer_out = lax.psum_scatter(
        partial_value.astype(jnp.bfloat16), "head", scatter_dimension=1, tiled=True
    )
    full_grad = lax.all_gather(grad_out, "head", axis=1, tiled=True)
    piece = lax.all_gather(w_out, "seq", axis=1, tiled=True)
    cols = full_grad
    back = jnp.einsum("tr,kr->tk", cols, piece, preferred_element_type=jnp.float32)
    grad_gated = lax.optimization_barrier(back.astype(jnp.bfloat16))
    out_term = jnp.einsum("tk,td->kd", gated, full_grad, preferred_element_type=jnp.float32)
    grad_wout = lax.psum_scatter(
        out_term.astype(jnp.bfloat16), "seq", scatter_dimension=1, tiled=True
    ).astype(jnp.float32)
    upstream = grad_gated.astype(jnp.float32)
    gain_part = jnp.sum(upstream * mixed * rinv[:, None], axis=0)
    inner = lax.psum(jnp.sum(upstream * norm_gain[None] * mixed, axis=1), "head")
    grad_mixed = (
        rinv[:, None] * norm_gain[None] * upstream
        - mixed * (rinv * rinv * rinv * inner / wide)[:, None]
    )
    first = pull_mixer(grad_mixed)
    ds_in = first[6]
    carried = carried_in((decay, ds_in), "seq", combine, identity)[1]
    grad_log = decay * jnp.sum(carried * s_in, axis=(1, 2))
    second = pull_states((carried, grad_log))
    d_zx = (first[0] + second[0]).reshape(tokens, -1).astype(jnp.bfloat16)
    d_dtr = (first[1] + second[1]).astype(jnp.bfloat16)
    d_bc = (first[2] + second[2]).reshape(tokens, -1)
    bc_upper, bc_lower = split_pair(d_bc)
    grad_dtbias, grad_alog, grad_dskip, grad_gain = lax.psum(
        (first[3] + second[3], first[4] + second[4], first[5], gain_part), "seq"
    )
    term = input_rows_term(
        (d_zx, d_dtr, bc_upper, bc_lower),
        lax.all_gather((w_zx, w_dt, w_bc), "seq", axis=0, tiled=True),
    )
    grad_hidden = lax.psum_scatter(
        term.astype(jnp.bfloat16), "head", scatter_dimension=1, tiled=True
    )
    bc_total = lax.psum(d_bc.astype(jnp.bfloat16), "head").astype(jnp.float32)
    total_upper, total_lower = split_pair(bc_total)
    cols = full_in
    bc_term = jnp.einsum(
        "tr,tc->rc", cols, total_upper, preferred_element_type=jnp.float32
    ) + jnp.einsum("tr,tc->rc", cols, total_lower, preferred_element_type=jnp.float32)
    sums = lax.psum_scatter(
        jnp.concatenate(
            [
                jnp.einsum("tr,tc->rc", cols, d_zx, preferred_element_type=jnp.float32),
                jnp.einsum("tr,th->rh", cols, d_dtr, preferred_element_type=jnp.float32),
                bc_term,
            ],
            axis=1,
        ).astype(jnp.bfloat16),
        "seq",
        scatter_dimension=0,
        tiled=True,
    ).astype(jnp.float32)
    rows_here = w_zx.shape[0]
    grad_wzx = sums[:, :local_cols].reshape(rows_here, 2, -1)
    grad_wdt = sums[:, local_cols : local_cols + head_cols]
    grad_wbc = sums[:, local_cols + head_cols :].reshape(rows_here, 2, -1)
    return (
        layer_out,
        grad_hidden,
        grad_wzx,
        grad_wdt,
        grad_wbc,
        grad_dtbias,
        grad_alog,
        grad_dskip,
        grad_gain,
        grad_wout,
    )


def mixer_cols(z_t, xr_t, dtr_t, b_t, c_t, dt_bias, a_log, d_skip):
    nheads, rows = dtr_t.shape
    blocks = rows // BLOCK
    width = xr_t.shape[0] // nheads
    pos = jnp.arange(BLOCK)
    lower = pos[:, None] >= pos[None, :]
    x = jax.nn.silu(xr_t).reshape(nheads, width, blocks, BLOCK)
    dt = jax.nn.softplus(dtr_t + dt_bias[:, None])
    ld = (-dt * jnp.exp(a_log)[:, None]).reshape(nheads, blocks, BLOCK)
    dt = dt.reshape(nheads, blocks, BLOCK)
    cumul = jnp.einsum("hks,ts->hkt", ld, lower.astype(jnp.float32), precision=HIGH)
    tail = cumul[:, :, -1]
    b_blk = b_t.reshape(-1, blocks, BLOCK)
    c_blk = c_t.reshape(-1, blocks, BLOCK)
    scores = jnp.einsum("nkt,nks->kts", c_blk, b_blk, precision=MID)
    gaps = cumul[:, :, :, None] - cumul[:, :, None, :]
    weights = jnp.exp(jnp.where(lower, gaps, -1e30)) * scores[None] * dt[:, :, None, :]
    y = jnp.einsum("hkts,hpks->hpkt", weights, x, precision=MID)
    inflow = jnp.exp(tail[:, :, None] - cumul) * dt
    fresh = jnp.einsum("hpks,nks->hkpn", x * inflow[:, None], b_blk, precision=MID)
    at = jnp.arange(blocks)
    reach = (at[:, None] > at[None, :]).astype(jnp.float32)
    ahead = jnp.einsum("hj,kj->hk", tail, reach, precision=HIGH)
    span = ahead[:, :, None] - (ahead + tail)[:, None, :]
    carry = jnp.exp(jnp.where(at[:, None] > at[None, :], span, -1e30))
    state = jnp.einsum("hkj,hjpn->hkpn", carry, fresh, precision=HIGH)
    y = y + jnp.einsum("nkt,hkpn->hpkt", c_blk, state, precision=MID) * jnp.exp(cumul)[:, None]
    y = y + d_skip[:, None, None, None] * x
    return y.reshape(nheads * width, rows) * jax.nn.silu(z_t)


def shifted(x, k):
    count = lax.axis_size("head")
    return lax.ppermute(x, "head", [(i, (i + k) % count) for i in range(count)])


def head_gather(x):
    count, h = lax.axis_size("head"), lax.axis_index("head")
    rows = x.shape[0]
    whole = jnp.zeros((count * rows,) + x.shape[1:], x.dtype)
    for k in range(count):
        part = shifted(x, k) if k else x
        whole = lax.dynamic_update_slice_in_dim(whole, part, lax.rem(h + count - k, count) * rows, 0)
    return whole


def head_sum(x, axis):
    count, h = lax.axis_size("head"), lax.axis_index("head")
    size = x.shape[axis] // count
    total = None
    for k in range(count):
        part = lax.dynamic_slice_in_dim(x, lax.rem(h + k, count) * size, size, axis)
        part = (shifted(part, k) if k else part).astype(jnp.float32)
        total = part if total is None else total + part
    return total


def activations_moved(hidden, w_zx, w_dt, w_bc, dt_bias, a_log, d_skip, norm_gain, w_out, grad_out):
    f32, bf16 = jnp.float32, jnp.bfloat16
    peers = lax.axis_size("seq")
    s, h = lax.axis_index("seq"), lax.axis_index("head")
    tokens = hidden.shape[0]
    rows = tokens * peers
    wide = HEADS * HDIM
    heads = w_dt.shape[1] // peers
    span = heads * HDIM
    states = w_bc.shape[2]
    chans = 2 * states // peers
    lines = chans * tokens // rows
    swap = [(a * peers + b, b * peers + a) for a in range(peers) for b in range(peers)]

    def turned(x):
        return lax.ppermute(x, ("seq", "head"), swap)

    def mine(x, size):
        return lax.dynamic_slice_in_dim(x, s * size, size, 0)

    w_z, w_x = w_zx[:, 0], w_zx[:, 1]
    w_b = w_bc.reshape(w_bc.shape[0], -1)
    hid = head_gather(turned(hidden))
    gout_rows, hid = lax.optimization_barrier((turned(grad_out), hid))
    gout = head_gather(gout_rows)

    def times_hidden(w, cols):
        return jnp.einsum("dc,td->ct", w, cols, preferred_element_type=f32)

    x_part = times_hidden(w_x, hid).reshape(peers, span, rows)
    hid_h = lax.dynamic_slice_in_dim(hid, h * tokens, tokens, 0)
    bc_part = times_hidden(w_b, hid_h).reshape(peers, lines, rows)
    dt_part = times_hidden(w_dt, hid).reshape(peers, heads, rows)
    dt_part = jnp.pad(dt_part, ((0, 0), (0, -heads % 16), (0, 0)))
    packed = jnp.concatenate([x_part, bc_part, dt_part], axis=1)
    packed, hid = lax.optimization_barrier((packed, hid))
    mixed_in = lax.psum_scatter(packed, "seq", scatter_dimension=0, tiled=True)[0]
    z_part = times_hidden(w_z, hid).reshape(peers, span, rows)
    up_part = jnp.einsum("kd,td->kt", w_out, gout, preferred_element_type=f32).astype(bf16)
    z_up = jnp.concatenate([z_part.astype(bf16), up_part.reshape(peers, span, rows)], axis=1)
    z_up = lax.psum_scatter(z_up, "seq", scatter_dimension=0, tiled=True)[0]
    z_b, up_b = z_up[:span], z_up[span:]
    mixed_in = mixed_in.astype(bf16)
    xr_b = mixed_in[:span]
    dtr_b = mixed_in[span + lines : span + lines + heads]
    bc_b = lax.all_gather(
        mixed_in[span : span + lines].reshape(chans, tokens), ("seq", "head"), axis=0
    )
    bc_b = bc_b.reshape(peers, -1, chans, tokens).transpose(0, 2, 1, 3).reshape(2, states, rows)
    bc_f = bc_b.astype(f32)
    bias, alog, skip = mine(dt_bias, heads), mine(a_log, heads), mine(d_skip, heads)
    gain = mine(norm_gain, span)[:, None]
    upstream = up_b.astype(f32)
    mixed, pull = jax.vjp(
        mixer_cols, z_b.astype(f32), xr_b.astype(f32), dtr_b.astype(f32),
        bc_f[0], bc_f[1], bias, alog, skip,
    )
    sums = jnp.stack([jnp.sum(mixed * mixed, axis=0), jnp.sum(upstream * gain * mixed, axis=0)])
    squares, inner = lax.psum(lax.psum(sums, "head"), "seq")
    rinv = lax.rsqrt(squares / wide + EPS_NORM)
    gated = (mixed * rinv[None] * gain).astype(bf16)
    grad_mixed = rinv[None] * gain * upstream - mixed * (rinv * rinv * rinv * inner / wide)[None]
    gain_part = jnp.sum(upstream * mixed * rinv[None], axis=1)
    d_z, d_xr, d_dtr, d_b, d_c, g_bias, g_alog, g_skip = pull(grad_mixed)
    first = lax.all_gather(jnp.concatenate([gated, d_z.astype(bf16)], axis=0), "seq", axis=0)
    gated_all = first[:, :span].reshape(peers * span, rows)
    dz_all = first[:, span:].reshape(peers * span, rows)
    d_bc_h = head_sum(jnp.concatenate([d_b, d_c], axis=0).astype(bf16), 1)
    small = jnp.concatenate([g_bias, g_alog, g_skip, gain_part])
    fill = -small.shape[0] % rows
    small = jnp.pad(small, (0, fill)).reshape(-1, rows)
    misc = jnp.concatenate([d_dtr.astype(bf16), *split_pair(small)], axis=0)
    misc = jnp.pad(misc, ((0, -misc.shape[0] % 16), (0, 0)))
    wave = jnp.concatenate(
        [d_xr.astype(bf16), d_bc_h.astype(bf16).reshape(-1, rows), misc], axis=0
    )
    waves = lax.all_gather(wave, "seq", axis=0)
    out_part = jnp.einsum("kt,kd->td", gated_all, w_out, preferred_element_type=f32)
    out_rows = head_sum(out_part.astype(bf16), 0).astype(bf16)
    out_rows, waves = lax.optimization_barrier((out_rows, waves))
    layer_out = turned(out_rows)
    dx_all = waves[:, :span].reshape(peers * span, rows)
    d_bc = jnp.sum(waves[:, span : span + peers * lines].astype(f32), axis=0)
    d_bc = d_bc.reshape(2 * states, tokens)
    rest = waves[:, span + peers * lines :]
    ddt_all = rest[:, :heads].reshape(peers * heads, rows)
    count = small.shape[0]
    pair = rest[:, heads : heads + 2 * count].astype(f32)
    small_all = (pair[:, :count] + pair[:, count:]).reshape(peers, -1)
    grad_dtbias, grad_alog, grad_dskip = (
        small_all[:, i * heads : (i + 1) * heads].reshape(-1) for i in range(3)
    )
    grad_gain = small_all[:, 3 * heads : 3 * heads + span].reshape(-1)

    grad_wout = jnp.dot(gated_all, gout, preferred_element_type=f32)

    hid_part = jnp.einsum("ct,dc->td", dz_all, w_z, preferred_element_type=f32)
    hid_part = hid_part + jnp.einsum("ct,dc->td", dx_all, w_x, preferred_element_type=f32)
    hid_part = hid_part + jnp.einsum("ct,dc->td", ddt_all, w_dt, preferred_element_type=f32)
    hid_rows = head_sum(hid_part.astype(bf16), 0)
    for part in split_pair(d_bc):
        hid_rows = hid_rows + jnp.einsum("ct,dc->td", part, w_b, preferred_element_type=f32)
    grad_wzx = jnp.stack(
        [jnp.einsum("td,ct->dc", hid, g, preferred_element_type=f32) for g in (dz_all, dx_all)],
        axis=1,
    )
    hid_rows, grad_wzx = lax.optimization_barrier((hid_rows.astype(bf16), grad_wzx))
    grad_hidden = turned(hid_rows)
    grad_wdt = jnp.einsum("td,ct->dc", hid, ddt_all, preferred_element_type=f32)
    bc_all = head_gather(d_bc.astype(bf16)).reshape(-1, 2 * states, tokens)
    grad_wbc = jnp.einsum(
        "htd,hct->dc", hid.reshape(-1, tokens, hid.shape[1]), bc_all, preferred_element_type=f32
    )
    return (
        layer_out,
        grad_hidden,
        grad_wzx,
        grad_wdt,
        grad_wbc.reshape(w_bc.shape),
        grad_dtbias,
        grad_alog,
        grad_dskip,
        grad_gain,
        grad_wout,
    )


def solution(mesh):
    seq, head = mesh.shape["seq"], mesh.shape["head"]
    even = seq == head and HEADS % (seq * head) == 0
    on_device = activations_moved if even else weights_moved
    in_specs = (
        P(("groups", "seq"), "head"),
        P("seq", None, "head"),
        P("seq", "head"),
        P("seq", None, None),
        P("head"),
        P("head"),
        P("head"),
        P("head"),
        P("head", "seq"),
        P(("groups", "seq"), "head"),
    )
    out_specs = (
        P(("groups", "seq"), "head"),
        P(("groups", "seq"), "head"),
        P(("groups", "seq"), None, "head"),
        P(("groups", "seq"), "head"),
        P(("groups", "seq"), None, None),
        P(("groups", "head")),
        P(("groups", "head")),
        P(("groups", "head")),
        P(("groups", "head")),
        P(("groups", "head"), "seq"),
    )
    return jax.shard_map(
        on_device, mesh=mesh, in_specs=in_specs, out_specs=out_specs, check_vma=False
    )
```
